256 devices in a mesh: seq: 32 (over y, z), dp: 8 (over x, core).
Axes of the slice: x: 4, y: 4, z: 8, core: 2. Of those that a mesh axis runs over, the one named last changes fastest.
Arguments:
- inputs: bfloat16 [8, 4096, 2048], P('dp', 'seq'), may hold values from -6 to 6
- query_rows: bfloat16 [8, 4096, 2048], P('dp', 'seq'), may hold values from -6 to 6
- key_rows: bfloat16 [8, 4096, 2048], P('dp', 'seq'), may hold values from -6 to 6
- cotangent: bfloat16 [8, 4096, 2048], P('dp', 'seq'), may hold values from -6 to 6
- w_value: bfloat16 [2048, 2048], P('seq'), may hold values from -0.125 to 0.125
Outputs:
- grad_query: bfloat16 [8, 4096, 2048], P('dp', 'seq')
- grad_key: bfloat16 [8, 4096, 2048], P('dp', 'seq')
- grad_weight: float32 [2048, 2048], P('seq')
The draws below stay inside these ranges and needn't reach their ends.
All inputs are finite; a program needn't handle non-finite values.
Results may differ from the reference program's by a relative error of at most 0.025.
Values may be sent and summed in bfloat16 or wider, within the bound.
No kernel may reach another device: no remote copies, remote signals or barrier semaphores. Data moves between devices by JAX's collectives and lax.ppermute only.
A program may use at most 192 MiB of HBM per device.

```python
import math
import jax
import jax.numpy as jnp
from jax import lax

D = 2048
HEADS = 16
HEAD = 128
T_DEV = 128
HD = 2048
LENGTH = 4096
BATCH = 8


def spiked(entries, stream_key, source, target, parts, factor):
    owner, partner = [(jnp.arange(entries.shape[axis_at]) // (entries.shape[axis_at] // parts)).reshape([-1 if axis == axis_at else 1 for axis in range(entries.ndim)]) for axis_at in (source, target)]
    chosen = jax.random.permutation(stream_key, parts)[partner]
    strong = (owner == chosen) | (owner == (partner + parts // 2) % parts)
    return jnp.where(strong, factor * entries, entries)


def block_levels(rng, extent, pieces, low, top_value):
    factor_of, own = 1.0, jax.random.fold_in(rng, 6)
    for axis_at, blocks in pieces:
        steps = jnp.exp(jax.random.uniform(jax.random.fold_in(own, axis_at), (blocks,), jnp.float32, low / len(pieces), top_value / len(pieces)))
        factor_of = factor_of * jnp.repeat(steps, extent[axis_at] // blocks).reshape([-1 if axis == axis_at else 1 for axis in range(len(extent))])
    return factor_of


def gaussian(rng, dims, width, bound, cuts=(), held_as=jnp.bfloat16):
    factor_of = block_levels(rng, dims, cuts, -0.22, 0.18) if cuts else 1.0
    drawn = jax.random.normal(rng, dims, jnp.float32) * width * factor_of
    return jnp.minimum(jnp.maximum(drawn, -bound), bound).astype(held_as)


def bell_draw_with(rng, extent, scale, most, pieces, heavy, kind=jnp.bfloat16):
    array = scale * jax.random.normal(rng, extent, jnp.float32)
    if pieces:
        array = array * block_levels(rng, extent, pieces, -0.22, 0.18)
    return jnp.clip(spiked(array, jax.random.fold_in(rng, 3), *heavy), -most, most).astype(kind)


def setup_inputs(seed: int = 0) -> dict:
    keys = jax.random.split(jax.random.key(seed), 6)
    inputs = bell_draw_with(keys[0], (BATCH, LENGTH, D), 1.0, 6.0, ((0, 8), (1, 32)), (1, 2, 32, 2.75))
    query_rows = gaussian(keys[1], (BATCH, LENGTH, HD), 1.0, 6.0, ((0, 8), (1, 32)))
    key_rows = gaussian(keys[2], (BATCH, LENGTH, HD), 1.0, 6.0, ((0, 8), (1, 32)))
    cotangent = gaussian(keys[3], (BATCH, LENGTH, HD), 1.0, 6.0, ((0, 8), (1, 32)))
    w_value = gaussian(keys[4], (D, HD), D ** -0.5, 0.125, ((0, 32),))
    return dict(inputs=inputs, query_rows=query_rows, key_rows=key_rows, cotangent=cotangent, w_value=w_value)


def reference(inputs, query_rows, key_rows, cotangent, w_value):
    blocks_count = LENGTH // T_DEV
    width_all = HEADS * HEAD
    scale = 1.0 / math.sqrt(HEAD * LENGTH)
    grad_scale = 1.0 / math.sqrt(BATCH * LENGTH)
    flat_inputs = inputs.reshape(BATCH * LENGTH, D)
    values = jnp.dot(flat_inputs, w_value, preferred_element_type=jnp.float32).astype(jnp.bfloat16)
    values = values.reshape(BATCH, LENGTH, width_all)

    def split_blocks(array_in):
        return array_in.reshape(BATCH, blocks_count, T_DEV, HEADS, HEAD)
    positions = jnp.arange(T_DEV, dtype=jnp.int32)
    causal = positions[:, None] >= positions[None, :]

    def one_block(piece):
        q_one, k_one, v_one, g_one, kv_prior, qg_later = piece
        float_q = q_one.astype(jnp.float32)
        float_k = k_one.astype(jnp.float32)
        float_v = v_one.astype(jnp.float32)
        float_g = g_one.astype(jnp.float32)
        score_gv = jnp.einsum('thd,shd->hts', float_g, float_v) * scale
        score_gv = jnp.where(causal[None], score_gv, 0.0).astype(jnp.bfloat16).astype(jnp.float32)
        score_qk = jnp.einsum('thd,shd->hts', float_q, float_k) * scale
        score_qk = jnp.where(causal[None], score_qk, 0.0).astype(jnp.bfloat16).astype(jnp.float32)
        kv_round = kv_prior.astype(jnp.bfloat16).astype(jnp.float32)
        qg_round = qg_later.astype(jnp.bfloat16).astype(jnp.float32)
        grad_q = scale * jnp.einsum('the,hde->thd', float_g, kv_round) + jnp.einsum('hts,shd->thd', score_gv, float_k)
        grad_k = scale * jnp.einsum('she,hde->shd', float_v, qg_round) + jnp.einsum('hts,thd->shd', score_gv, float_q)
        grad_v = scale * jnp.einsum('shd,hde->she', float_k, qg_round) + jnp.einsum('hts,the->she', score_qk, float_g)
        return (grad_q.astype(jnp.bfloat16), grad_k.astype(jnp.bfloat16), grad_v.astype(jnp.bfloat16))

    def one_sequence(item):
        q_seq, k_seq, v_seq, g_seq = item
        kv_block = jnp.einsum('jthd,jthe->jhde', k_seq.astype(jnp.float32), v_seq.astype(jnp.float32))
        qg_block = jnp.einsum('jthd,jthe->jhde', q_seq.astype(jnp.float32), g_seq.astype(jnp.float32))
        kv_sum = jnp.cumsum(kv_block, axis=0)
        kv_before = jnp.concatenate([jnp.zeros_like(kv_block[:1]), kv_sum[:-1]], axis=0)
        qg_sum = jnp.cumsum(qg_block[::-1], axis=0)[::-1]
        qg_after = jnp.concatenate([qg_sum[1:], jnp.zeros_like(qg_block[:1])], axis=0)
        return lax.map(one_block, (q_seq, k_seq, v_seq, g_seq, kv_before, qg_after))
    grad_q, grad_k, grad_v = lax.map(one_sequence, (split_blocks(query_rows), split_blocks(key_rows), split_blocks(values), split_blocks(cotangent)))
    grad_q = grad_q.reshape(BATCH, LENGTH, width_all)
    grad_k = grad_k.reshape(BATCH, LENGTH, width_all)
    grad_v = grad_v.reshape(BATCH * LENGTH, width_all)
    grad_weight = lax.dot_general(flat_inputs, grad_v, (((0,), (0,)), ((), ())), preferred_element_type=jnp.float32) * grad_scale
    return (grad_q, grad_k, grad_weight)
```

```python
import functools
import math

import jax
import jax.numpy as jnp
from jax import lax
from jax.experimental import pallas as pl
from jax.experimental.pallas import tpu as pltpu
from jax.sharding import PartitionSpec as P

HEAD = 128
F32 = jnp.float32
BF16 = jnp.bfloat16


def dot(a, b, a_dim, b_dim):
    return lax.dot_general(a, b, (((a_dim,), (b_dim,)), ((), ())), preferred_element_type=F32)


def cols(h):
    return slice(h * HEAD, (h + 1) * HEAD)


def state_kernel(left_ref, right_ref, out_ref):
    for h in range(left_ref.shape[1] // HEAD):
        out_ref[cols(h), :] = dot(left_ref[:, cols(h)], right_ref[:, cols(h)], 0, 0).astype(BF16)


def block_state_kernel(left_ref, right_ref, out_ref):
    per = right_ref.shape[2] // HEAD
    for h in range(left_ref.shape[1] // HEAD):
        right = right_ref[h // per, :, cols(h % per)]
        out_ref[cols(h), :] = dot(left_ref[:, cols(h)], right, 0, 0).astype(BF16)


def prefix_kernel(reverse, part_ref, out_ref):
    count = part_ref.shape[0]
    total = jnp.zeros(part_ref.shape[1:], F32)
    for step in range(count):
        i = count - 1 - step if reverse else step
        out_ref[i] = total.astype(BF16)
        total = total + part_ref[i].astype(F32)


def causal_mask(rows):
    t = lax.broadcasted_iota(jnp.int32, (rows, rows), 0)
    s = lax.broadcasted_iota(jnp.int32, (rows, rows), 1)
    return t >= s


def grad_values_kernel(scale, q_ref, k_ref, g_ref, qg_ref, out_ref):
    mask = causal_mask(q_ref.shape[0])
    per = out_ref.shape[2] // HEAD
    for h in range(q_ref.shape[1] // HEAD):
        q, k, g = q_ref[:, cols(h)], k_ref[:, cols(h)], g_ref[:, cols(h)]
        score = jnp.where(mask, dot(q, k, 1, 1) * scale, 0.0).astype(BF16)
        grad = scale * dot(k, qg_ref[cols(h), :], 1, 0) + dot(score, g, 0, 0)
        out_ref[h // per, :, cols(h % per)] = grad.astype(BF16)


def grad_rows_kernel(scale, q_ref, k_ref, g_ref, v_ref, kv_ref, qg_ref, gq_ref, gk_ref):
    mask = causal_mask(q_ref.shape[0])
    per = v_ref.shape[2] // HEAD
    for h in range(q_ref.shape[1] // HEAD):
        q, k, g = q_ref[:, cols(h)], k_ref[:, cols(h)], g_ref[:, cols(h)]
        v = v_ref[h // per, :, cols(h % per)]
        score = jnp.where(mask, dot(g, v, 1, 1) * scale, 0.0).astype(BF16)
        grad_q = scale * dot(g, kv_ref[cols(h), :], 1, 1) + dot(score, k, 1, 0)
        gq_ref[:, cols(h)] = grad_q.astype(BF16)
        grad_k = scale * dot(v, qg_ref[cols(h), :], 1, 1) + dot(score, q, 0, 0)
        gk_ref[:, cols(h)] = grad_k.astype(BF16)


def reduce_kernel(factor, part_ref, out_ref):
    total = part_ref[0].astype(F32)
    for i in range(1, part_ref.shape[0]):
        total = total + part_ref[i].astype(F32)
    out_ref[...] = total * factor


def call(kernel, shapes, flops, *operands):
    out = [jax.ShapeDtypeStruct(s, d) for s, d in shapes]
    moved = sum(x.size * x.dtype.itemsize for x in list(operands) + out)
    result = pl.pallas_call(
        kernel,
        out_shape=out,
        in_specs=[pl.BlockSpec(memory_space=pltpu.VMEM)] * len(operands),
        out_specs=[pl.BlockSpec(memory_space=pltpu.VMEM)] * len(out),
        compiler_params=pltpu.CompilerParams(vmem_limit_bytes=24 * 2**20),
        cost_estimate=pl.CostEstimate(flops=flops, bytes_accessed=moved, transcendentals=0),
    )(*operands)
    return result[0] if len(result) == 1 else result


def on_device(inputs, query_rows, key_rows, cotangent, w_value):
    rows, width = inputs.shape[1:]
    width_all = query_rows.shape[2]
    heads = width_all // HEAD
    seq, dp = lax.axis_size("seq"), lax.axis_size("dp")
    scale = 1.0 / math.sqrt(HEAD * rows * seq)
    grad_scale = 1.0 / math.sqrt(inputs.shape[0] * dp * rows * seq)
    block = width_all // dp
    q, k, g = query_rows[0], key_rows[0], cotangent[0]
    head_flops = 2 * rows * HEAD * HEAD * heads

    def exchange(array, axis):
        return lax.all_to_all(array, axis, 0, 0, tiled=True)

    def carried(state, reverse):
        parts = exchange(state.reshape(seq, -1, HEAD), "seq")
        sums = call(
            functools.partial(prefix_kernel, reverse), [(parts.shape, BF16)], parts.size, parts
        )
        return exchange(sums, "seq").reshape(state.shape)

    all_inputs = lax.all_gather(inputs, "dp", axis=0, tiled=True).reshape(dp * rows, width)
    own = lax.dynamic_slice_in_dim(w_value, lax.axis_index("dp") * block, block, 1)
    columns = exchange(jnp.broadcast_to(own[None], (seq,) + own.shape), "seq").reshape(width, block)

    qg_local = call(state_kernel, [((heads * HEAD, HEAD), BF16)], head_flops, q, g)
    qg_round = carried(qg_local, True)

    values = jnp.dot(all_inputs, columns, preferred_element_type=F32).astype(BF16)
    values = exchange(values.reshape(dp, rows, block), "dp")
    kv_local = call(block_state_kernel, [((heads * HEAD, HEAD), BF16)], head_flops, k, values)
    kv_round = carried(kv_local, False)

    grad_values = call(
        functools.partial(grad_values_kernel, scale),
        [((dp, rows, block), BF16)], 3 * head_flops, q, k, g, qg_round,
    )
    grad_values = exchange(grad_values, "dp").reshape(dp * rows, block)
    product = dot(all_inputs, grad_values, 0, 0).astype(BF16)
    parts = exchange(product.reshape(seq, width // seq, block), "seq")
    summed = call(
        functools.partial(reduce_kernel, grad_scale), [(parts.shape[1:], F32)], parts.size, parts
    )
    grad_weight = lax.all_gather(summed, "dp", axis=1, tiled=True)

    grad_query, grad_key = call(
        functools.partial(grad_rows_kernel, scale),
        [((rows, width_all), BF16)] * 2, 5 * head_flops, q, k, g, values, kv_round, qg_round,
    )
    return grad_query[None], grad_key[None], grad_weight


def solution(mesh):
    placed = (
        P("dp", "seq", None),
        P("dp", "seq", None),
        P("dp", "seq", None),
        P("dp", "seq", None),
        P("seq", None),
    )
    return jax.shard_map(
        on_device,
        mesh=mesh,
        in_specs=placed,
        out_specs=(P("dp", "seq", None), P("dp", "seq", None), P("seq", None)),
        check_vma=False,
    )
```

```python
import functools
import math

import jax
import jax.numpy as jnp
from jax import lax
from jax.experimental import pallas as pl
from jax.experimental.pallas import tpu as pltpu
from jax.sharding import PartitionSpec as P

HEAD = 128
F32 = jnp.float32
BF16 = jnp.bfloat16


def dot(a, b, a_dim, b_dim):
    return lax.dot_general(a, b, (((a_dim,), (b_dim,)), ((), ())), preferred_element_type=F32)


def cols(h):
    return slice(h * HEAD, (h + 1) * HEAD)


def span(index, size):
    return pl.ds(pl.multiple_of(index * size, size), size)


def causal_mask(rows):
    t = lax.broadcasted_iota(jnp.int32, (rows, rows), 0)
    s = lax.broadcasted_iota(jnp.int32, (rows, rows), 1)
    return t >= s


def first_kernel(ids, q_ref, g_ref, w_ref, out_ref):
    count, rows, _ = out_ref.shape
    for h in range(q_ref.shape[1] // HEAD):
        state = dot(q_ref[:, cols(h)], g_ref[:, cols(h)], 0, 0).astype(BF16)
        for i in range(HEAD // rows):
            out_ref[h * (HEAD // rows) + i, :, :HEAD] = state[i * rows:(i + 1) * rows, :]
    block = out_ref.shape[2] - HEAD
    own = w_ref[:, span(ids[0], block)]
    for i in range(count):
        out_ref[i, :, HEAD:] = own


def slot_state_kernel(slots, ids, left_ref, *refs):
    rights, (out_ref, whole_ref) = refs[:slots], refs[-2:]
    block = rights[0].shape[1]
    for o, right_ref in enumerate(rights):
        b = ids[0] ^ o
        left = left_ref[:, span(b, block)]
        whole_ref[:, span(b, block)] = right_ref[...]
        for j in range(block // HEAD):
            state = dot(left[:, cols(j)], right_ref[:, cols(j)], 0, 0).astype(BF16)
            out_ref[span(b * (block // HEAD) + j, HEAD), :] = state


def prefix_kernel(reverse, ids, part_ref, *refs):
    out_ref = refs[-1]
    count = part_ref.shape[0]
    total = jnp.zeros(out_ref.shape[1:], F32)
    for step in range(count):
        i = count - 1 - step if reverse else step
        out_ref[i] = total.astype(BF16)
        total = total + part_ref[i, :, :HEAD].astype(F32)


def values_kernel(slots, ids, x_ref, first_ref, *refs):
    outs, (w_ref, res_ref) = refs[-slots - 2:-2], refs[-2:]
    step = pl.program_id(0)
    count, rows = x_ref.shape[:2]

    @pl.when(step == 0)
    def _():
        size = first_ref.shape[1]
        for i in range(first_ref.shape[0]):
            w_ref[i * size:(i + 1) * size, :] = first_ref[i, :, HEAD:]

    x = x_ref[...].reshape(count * rows, x_ref.shape[2])
    res_ref[...] = dot(x, w_ref[...], 1, 0).astype(BF16).reshape(res_ref.shape)
    for o, out_ref in enumerate(outs):
        @pl.when(step == o // count)
        def _(o=o, out_ref=out_ref):
            out_ref[...] = res_ref[(ids[0] ^ o) % count]


def grad_values_kernel(scale, slots, ids, q_ref, k_ref, g_ref, qg_ref, *refs):
    outs = refs[-slots:]
    mask = causal_mask(q_ref.shape[0])
    block = outs[0].shape[1]
    for o, out_ref in enumerate(outs):
        b = ids[0] ^ o
        at = span(b, block)
        qs, ks, gs = q_ref[:, at], k_ref[:, at], g_ref[:, at]
        for j in range(block // HEAD):
            q, k, g = qs[:, cols(j)], ks[:, cols(j)], gs[:, cols(j)]
            state = qg_ref[span(b * (block // HEAD) + j, HEAD), :]
            score = jnp.where(mask, dot(q, k, 1, 1) * scale, 0.0).astype(BF16)
            grad = scale * dot(k, state, 1, 0) + dot(score, g, 0, 0)
            out_ref[:, cols(j)] = grad.astype(BF16)


def grad_key_kernel(scale, ids, q_ref, g_ref, v_ref, qg_ref, *refs):
    gk_ref, score_ref = refs[-2:]
    mask = causal_mask(q_ref.shape[0])
    for h in range(q_ref.shape[1] // HEAD):
        q, g, v = q_ref[:, cols(h)], g_ref[:, cols(h)], v_ref[:, cols(h)]
        score = jnp.where(mask, dot(g, v, 1, 1) * scale, 0.0).astype(BF16)
        score_ref[cols(h), :] = score
        grad = scale * dot(v, qg_ref[cols(h), :], 1, 1) + dot(score, q, 0, 0)
        gk_ref[:, cols(h)] = grad.astype(BF16)


def grad_query_kernel(scale, ids, k_ref, g_ref, score_ref, kv_ref, gq_ref):
    for h in range(k_ref.shape[1] // HEAD):
        grad = scale * dot(g_ref[:, cols(h)], kv_ref[cols(h), :], 1, 1)
        grad = grad + dot(score_ref[cols(h), :], k_ref[:, cols(h)], 1, 0)
        gq_ref[:, cols(h)] = grad.astype(BF16)


def product_kernel(slots, ids, x_ref, *refs):
    pieces, out_ref, held_ref = refs[:slots], refs[-2], refs[-1]

    @pl.when(pl.program_id(0) == 0)
    def _():
        for o, piece in enumerate(pieces):
            held_ref[:, span(ids[0] ^ o, piece.shape[0])] = piece[...].T

    out_ref[0] = dot(held_ref[...], x_ref[...], 1, 0).astype(BF16).T


def parts_sum_kernel(factor, ids, part_ref, *refs):
    total = part_ref[0].astype(F32)
    for i in range(1, part_ref.shape[0]):
        total = total + part_ref[i].astype(F32)
    refs[-1][...] = (total * factor).astype(BF16)


def assemble_kernel(ids, part_ref, out_ref):
    block = part_ref.shape[2]
    for b in range(part_ref.shape[0]):
        out_ref[:, b * block:(b + 1) * block] = part_ref[b].astype(F32)


def call(kernel, shapes, flops, ids, *operands, grid=None, first=None, out_first=None, scratch=(), after=(), through=()):
    out = [jax.ShapeDtypeStruct(s, d) for s, d in shapes]
    moved = sum(x.size * x.dtype.itemsize for x in list(operands) + out)
    whole = lambda s: pl.BlockSpec(s, lambda *_: (0,) * len(s))
    anywhere = pl.BlockSpec(memory_space=pl.ANY)
    in_specs = [whole(x.shape) for x in operands]
    if first is not None:
        in_specs[0] = first
    out_specs = [out_first] if out_first else [whole(s) for s, _ in shapes]
    result = pl.pallas_call(
        kernel,
        out_shape=[jax.ShapeDtypeStruct(x.shape, x.dtype) for x in through] + out,
        grid_spec=pltpu.PrefetchScalarGridSpec(
            num_scalar_prefetch=1,
            grid=grid or (1,),
            in_specs=in_specs + [anywhere] * (len(after) + len(through)),
            out_specs=[anywhere] * len(through) + out_specs,
            scratch_shapes=list(scratch),
        ),
        input_output_aliases={1 + len(operands) + len(after) + i: i for i in range(len(through))},
        compiler_params=pltpu.CompilerParams(vmem_limit_bytes=16 * 2**20),
        cost_estimate=pl.CostEstimate(flops=flops, bytes_accessed=moved, transcendentals=0),
    )(ids, *operands, *after, *through)
    return result[0] if len(result) == 1 else result


def on_device(inputs, query_rows, key_rows, cotangent, w_value):
    rows, width = inputs.shape[1:]
    width_all = query_rows.shape[2]
    heads = width_all // HEAD
    seq, dp = lax.axis_size("seq"), lax.axis_size("dp")
    pieces = 4
    scale = 1.0 / math.sqrt(HEAD * rows * seq)
    grad_scale = 1.0 / math.sqrt(inputs.shape[0] * dp * rows * seq)
    block = width_all // dp
    q, k, g = query_rows[0], key_rows[0], cotangent[0]
    head_flops = 2 * rows * HEAD * HEAD * heads
    ids = lax.axis_index("dp").astype(jnp.int32)[None]


    def exchange(array):
        return lax.all_to_all(array, "seq", 0, 0, tiled=True)

    def swap_slots(arrays):
        return [
            a if o == 0 else lax.ppermute(a, "dp", [(i, i ^ o) for i in range(dp)])
            for o, a in enumerate(arrays)
        ]

    def sums_of(parts, reverse, through=()):
        return call(
            functools.partial(prefix_kernel, reverse), [((seq, width_all // seq, HEAD), BF16)],
            seq * width_all // seq * HEAD, ids, parts, through=through,
        )

    all_inputs = lax.all_gather(inputs, "dp", axis=0, tiled=True)

    first = exchange(call(
        first_kernel, [((seq, width // seq, HEAD + block), BF16)], head_flops, ids, q, g, w_value
    ))
    qg_sums = sums_of(first, True)
    qg_round = exchange(qg_sums).reshape(width_all, HEAD)

    values = call(
        functools.partial(values_kernel, dp), [((rows, block), BF16)] * dp,
        2 * rows * width * width_all, ids, all_inputs, first, after=(qg_sums,),
        grid=(dp // 2,),
        first=pl.BlockSpec((2, rows, width), lambda i, ids: ((ids[0] // 2) ^ i, 0, 0)),
        scratch=[pltpu.VMEM((width, block), BF16), pltpu.VMEM((2, rows, block), BF16)],
    )
    kv_local, values = call(
        functools.partial(slot_state_kernel, dp),
        [((heads * HEAD, HEAD), BF16), ((rows, width_all), BF16)], head_flops, ids, k,
        *swap_slots(values), after=(qg_round,),
    )
    kv_parts = exchange(kv_local.reshape(seq, -1, HEAD))

    grad_values = call(
        functools.partial(grad_values_kernel, scale, dp), [((rows, block), BF16)] * dp,
        3 * head_flops, ids, q, k, g, qg_round, after=(kv_local,),
    )
    terms = call(
        functools.partial(product_kernel, dp), [((pieces, width // pieces, block), BF16)],
        2 * rows * width * width_all, ids, all_inputs.reshape(dp * rows, width),
        *swap_slots(grad_values),
        grid=(pieces,),
        first=pl.BlockSpec((dp * rows, width // pieces), lambda i, ids: (0, i)),
        out_first=pl.BlockSpec((1, width // pieces, block), lambda i, ids: (i, 0, 0)),
        scratch=[pltpu.VMEM((block, dp * rows), BF16)],
    )
    terms, kv_sums = sums_of(kv_parts, False, (terms,))
    grad_key, score = call(
        functools.partial(grad_key_kernel, scale),
        [((rows, width_all), BF16), ((heads * HEAD, rows), BF16)],
        3 * head_flops, ids, q, g, values, qg_round, after=(kv_sums,),
    )
    parts = exchange(terms.reshape(seq, width // seq, block))
    kv_sums, summed = call(
        functools.partial(parts_sum_kernel, grad_scale), [((width // seq, block), BF16)],
        0, ids, parts, after=(score,), through=(kv_sums,),
    )
    kv_round = exchange(kv_sums).reshape(width_all, HEAD)
    grad_weight = call(
        assemble_kernel, [((width // seq, width_all), F32)], 0, ids, lax.all_gather(summed, "dp")
    )

    grad_query = call(
        functools.partial(grad_query_kernel, scale), [((rows, width_all), BF16)],
        2 * head_flops, ids, k, g, score, kv_round,
    )
    return grad_query[None], grad_key[None], grad_weight


def solution(mesh):
    placed = (
        P("dp", "seq", None),
        P("dp", "seq", None),
        P("dp", "seq", None),
        P("dp", "seq", None),
        P("seq", None),
    )
    return jax.shard_map(
        on_device,
        mesh=mesh,
        in_specs=placed,
        out_specs=(P("dp", "seq", None), P("dp", "seq", None), P("seq", None)),
        check_vma=False,
    )
```

```python
import functools
import math

import jax
import jax.numpy as jnp
from jax import lax
from jax.experimental import pallas as pl
from jax.experimental.pallas import tpu as pltpu
from jax.sharding import PartitionSpec as P

HEAD = 128
Z = 8
F32 = jnp.float32
BF16 = jnp.bfloat16


def dot(a, b, a_dim, b_dim):
    return lax.dot_general(a, b, (((a_dim,), (b_dim,)), ((), ())), preferred_element_type=F32)


def cols(h):
    return slice(h * HEAD, (h + 1) * HEAD)


def span(index, size):
    return pl.ds(pl.multiple_of(index * size, size), size)


def causal_mask(rows):
    t = lax.broadcasted_iota(jnp.int32, (rows, rows), 0)
    s = lax.broadcasted_iota(jnp.int32, (rows, rows), 1)
    return t >= s


def first_kernel(ids, q_ref, g_ref, w_ref, out_ref):
    count, rows, _ = out_ref.shape
    for h in range(q_ref.shape[1] // HEAD):
        state = dot(q_ref[:, cols(h)], g_ref[:, cols(h)], 0, 0).astype(BF16)
        for i in range(HEAD // rows):
            out_ref[h * (HEAD // rows) + i, :, :HEAD] = state[i * rows:(i + 1) * rows, :]
    block = out_ref.shape[2] - HEAD
    own = w_ref[:, span(ids[0], block)]
    for i in range(count):
        out_ref[i, :, HEAD:] = own


def slot_state_kernel(slots, ids, left_ref, *refs):
    rights, (out_ref, whole_ref) = refs[:slots], refs[-2:]
    block = rights[0].shape[1]
    for o, right_ref in enumerate(rights):
        b = ids[0] ^ o
        left = left_ref[:, span(b, block)]
        whole_ref[:, span(b, block)] = right_ref[...]
        for j in range(block // HEAD):
            state = dot(left[:, cols(j)], right_ref[:, cols(j)], 0, 0).astype(BF16)
            out_ref[span(b * (block // HEAD) + j, HEAD), :] = state


def prefix_kernel(reverse, ids, part_ref, *refs):
    out_ref = refs[-1]
    count = part_ref.shape[0]
    total = jnp.zeros(out_ref.shape[1:], F32)
    for step in range(count):
        i = count - 1 - step if reverse else step
        out_ref[i] = total.astype(BF16)
        total = total + part_ref[i, :, :HEAD].astype(F32)


def values_kernel(slots, ids, x_ref, first_ref, *refs):
    outs, (w_ref, res_ref) = refs[-slots - 2:-2], refs[-2:]
    step = pl.program_id(0)
    count, rows = x_ref.shape[:2]

    @pl.when(step == 0)
    def _():
        size = first_ref.shape[1]
        for i in range(first_ref.shape[0]):
            w_ref[i * size:(i + 1) * size, :] = first_ref[i, :, HEAD:]

    x = x_ref[...].reshape(count * rows, x_ref.shape[2])
    res_ref[...] = dot(x, w_ref[...], 1, 0).astype(BF16).reshape(res_ref.shape)
    for o, out_ref in enumerate(outs):
        @pl.when(step == o // count)
        def _(o=o, out_ref=out_ref):
            out_ref[...] = res_ref[(ids[0] ^ o) % count]


def grad_values_kernel(scale, slots, ids, q_ref, k_ref, g_ref, qg_ref, *refs):
    outs = refs[-slots:]
    mask = causal_mask(q_ref.shape[0])
    block = outs[0].shape[1]
    for o, out_ref in enumerate(outs):
        b = ids[0] ^ o
        at = span(b, block)
        qs, ks, gs = q_ref[:, at], k_ref[:, at], g_ref[:, at]
        for j in range(block // HEAD):
            q, k, g = qs[:, cols(j)], ks[:, cols(j)], gs[:, cols(j)]
            state = qg_ref[span(b * (block // HEAD) + j, HEAD), :]
            score = jnp.where(mask, dot(q, k, 1, 1) * scale, 0.0).astype(BF16)
            grad = scale * dot(k, state, 1, 0) + dot(score, g, 0, 0)
            out_ref[:, cols(j)] = grad.astype(BF16)


def grad_key_kernel(scale, ids, q_ref, g_ref, v_ref, qg_ref, *refs):
    gk_ref, score_ref = refs[-2:]
    mask = causal_mask(q_ref.shape[0])
    for h in range(q_ref.shape[1] // HEAD):
        q, g, v = q_ref[:, cols(h)], g_ref[:, cols(h)], v_ref[:, cols(h)]
        score = jnp.where(mask, dot(g, v, 1, 1) * scale, 0.0).astype(BF16)
        score_ref[cols(h), :] = score
        grad = scale * dot(v, qg_ref[cols(h), :], 1, 1) + dot(score, q, 0, 0)
        gk_ref[:, cols(h)] = grad.astype(BF16)


def grad_query_kernel(scale, ids, k_ref, g_ref, score_ref, kv_ref, gq_ref):
    for h in range(k_ref.shape[1] // HEAD):
        grad = scale * dot(g_ref[:, cols(h)], kv_ref[cols(h), :], 1, 1)
        grad = grad + dot(score_ref[cols(h), :], k_ref[:, cols(h)], 1, 0)
        gq_ref[:, cols(h)] = grad.astype(BF16)


def product_kernel(slots, ids, x_ref, *refs):
    pieces, out_ref, held_ref = refs[:slots], refs[-2], refs[-1]

    @pl.when(pl.program_id(0) == 0)
    def _():
        for o, piece in enumerate(pieces):
            held_ref[:, span(ids[0] ^ o, piece.shape[0])] = piece[...].T

    out_ref[0] = dot(held_ref[...], x_ref[...], 1, 0).astype(BF16).T


def parts_sum_kernel(factor, ids, part_ref, *refs):
    total = part_ref[0].astype(F32)
    for i in range(1, part_ref.shape[0]):
        total = total + part_ref[i].astype(F32)
    refs[-1][...] = (total * factor).astype(BF16)


def assemble_kernel(ids, part_ref, out_ref):
    block = part_ref.shape[2]
    for b in range(part_ref.shape[0]):
        out_ref[:, b * block:(b + 1) * block] = part_ref[b].astype(F32)


def call(kernel, shapes, flops, ids, *operands, grid=None, first=None, out_first=None, scratch=(), after=(), through=()):
    out = [jax.ShapeDtypeStruct(s, d) for s, d in shapes]
    moved = sum(x.size * x.dtype.itemsize for x in list(operands) + out)
    whole = lambda s: pl.BlockSpec(s, lambda *_: (0,) * len(s))
    anywhere = pl.BlockSpec(memory_space=pl.ANY)
    in_specs = [whole(x.shape) for x in operands]
    if first is not None:
        in_specs[0] = first
    out_specs = [out_first] if out_first else [whole(s) for s, _ in shapes]
    result = pl.pallas_call(
        kernel,
        out_shape=[jax.ShapeDtypeStruct(x.shape, x.dtype) for x in through] + out,
        grid_spec=pltpu.PrefetchScalarGridSpec(
            num_scalar_prefetch=1,
            grid=grid or (1,),
            in_specs=in_specs + [anywhere] * (len(after) + len(through)),
            out_specs=[anywhere] * len(through) + out_specs,
            scratch_shapes=list(scratch),
        ),
        input_output_aliases={1 + len(operands) + len(after) + i: i for i in range(len(through))},
        compiler_params=pltpu.CompilerParams(vmem_limit_bytes=16 * 2**20),
        cost_estimate=pl.CostEstimate(flops=flops, bytes_accessed=moved, transcendentals=0),
    )(ids, *operands, *after, *through)
    return result[0] if len(result) == 1 else result


def on_device(inputs, query_rows, key_rows, cotangent, w_value):
    rows, width = inputs.shape[1:]
    width_all = query_rows.shape[2]
    heads = width_all // HEAD
    seq, dp = lax.axis_size("seq"), lax.axis_size("dp")
    y_count = seq // Z
    planes = [[y * Z + z for z in range(Z)] for y in range(y_count)]
    columns = [[y * Z + z for y in range(y_count)] for z in range(Z)]
    scale = 1.0 / math.sqrt(HEAD * rows * seq)
    grad_scale = 1.0 / math.sqrt(inputs.shape[0] * dp * rows * seq)
    block = width_all // dp
    q, k, g = query_rows[0], key_rows[0], cotangent[0]
    head_flops = 2 * rows * HEAD * HEAD * heads
    ids = lax.axis_index("dp").astype(jnp.int32)[None]


    def exchange(array, groups=None):
        return lax.all_to_all(array, "seq", 0, 0, axis_index_groups=groups, tiled=True)

    def swap_slots(arrays):
        return [
            a if o == 0 else lax.ppermute(a, "dp", [(i, i ^ o) for i in range(dp)])
            for o, a in enumerate(arrays)
        ]

    def sums_of(parts, reverse, through=()):
        return call(
            functools.partial(prefix_kernel, reverse), [((seq, width_all // seq, HEAD), BF16)],
            seq * width_all // seq * HEAD, ids, parts, through=through,
        )

    all_inputs = lax.all_gather(inputs, "dp", axis=0, tiled=True)

    first = exchange(call(
        first_kernel, [((seq, width // seq, HEAD + block), BF16)], head_flops, ids, q, g, w_value
    ))
    qg_sums = sums_of(first, True)
    qg_round = exchange(qg_sums).reshape(width_all, HEAD)

    values = call(
        functools.partial(values_kernel, dp), [((rows, block), BF16)] * dp,
        2 * rows * width * width_all, ids, all_inputs, first, after=(qg_sums,),
        grid=(dp // 2,),
        first=pl.BlockSpec((2, rows, width), lambda i, ids: ((ids[0] // 2) ^ i, 0, 0)),
        scratch=[pltpu.VMEM((width, block), BF16), pltpu.VMEM((2, rows, block), BF16)],
    )
    kv_local, values = call(
        functools.partial(slot_state_kernel, dp),
        [((heads * HEAD, HEAD), BF16), ((rows, width_all), BF16)], head_flops, ids, k,
        *swap_slots(values), after=(qg_round,),
    )
    kv_parts = exchange(kv_local.reshape(seq, -1, HEAD))

    grad_values = call(
        functools.partial(grad_values_kernel, scale, dp), [((rows, block), BF16)] * dp,
        3 * head_flops, ids, q, k, g, qg_round, after=(kv_local,),
    )
    terms = call(
        functools.partial(product_kernel, dp), [((y_count, width // y_count, block), BF16)],
        2 * rows * width * width_all, ids, all_inputs.reshape(dp * rows, width),
        *swap_slots(grad_values),
        grid=(y_count,),
        first=pl.BlockSpec((dp * rows, width // y_count), lambda i, ids: (0, i)),
        out_first=pl.BlockSpec((1, width // y_count, block), lambda i, ids: (i, 0, 0)),
        scratch=[pltpu.VMEM((block, dp * rows), BF16)],
    )
    terms, kv_sums = sums_of(kv_parts, False, (terms,))
    grad_key, score = call(
        functools.partial(grad_key_kernel, scale),
        [((rows, width_all), BF16), ((heads * HEAD, rows), BF16)],
        3 * head_flops, ids, q, g, values, qg_round, after=(kv_sums,),
    )
    kv_round = exchange(kv_sums).reshape(width_all, HEAD)
    term = lax.psum_scatter(
        terms.reshape(width, block), "seq", scatter_dimension=0, axis_index_groups=columns, tiled=True
    )
    parts = exchange(term.reshape(Z, width // seq, block), planes)
    summed = call(
        functools.partial(parts_sum_kernel, grad_scale), [((width // seq, block), BF16)],
        0, ids, parts, after=(kv_round, score),
    )
    grad_weight = call(
        assemble_kernel, [((width // seq, width_all), F32)], 0, ids, lax.all_gather(summed, "dp")
    )

    grad_query = call(
        functools.partial(grad_query_kernel, scale), [((rows, width_all), BF16)],
        2 * head_flops, ids, k, g, score, kv_round,
    )
    return grad_query[None], grad_key[None], grad_weight


def solution(mesh):
    placed = (
        P("dp", "seq", None),
        P("dp", "seq", None),
        P("dp", "seq", None),
        P("dp", "seq", None),
        P("seq", None),
    )
    return jax.shard_map(
        on_device,
        mesh=mesh,
        in_specs=placed,
        out_specs=(P("dp", "seq", None), P("dp", "seq", None), P("seq", None)),
        check_vma=False,
    )
```

```python
import functools
import math

import jax
import jax.numpy as jnp
from jax import lax
from jax.experimental import pallas as pl
from jax.experimental.pallas import tpu as pltpu
from jax.sharding import PartitionSpec as P

HEAD = 128
Z = 8
F32 = jnp.float32
BF16 = jnp.bfloat16


def dot(a, b, a_dim, b_dim):
    return lax.dot_general(a, b, (((a_dim,), (b_dim,)), ((), ())), preferred_element_type=F32)


def cols(h):
    return slice(h * HEAD, (h + 1) * HEAD)


def span(index, size):
    return pl.ds(pl.multiple_of(index * size, size), size)


def causal_mask(rows):
    t = lax.broadcasted_iota(jnp.int32, (rows, rows), 0)
    s = lax.broadcasted_iota(jnp.int32, (rows, rows), 1)
    return t >= s


def state_kernel(ids, q_ref, g_ref, *refs):
    for h in range(q_ref.shape[1] // HEAD):
        refs[-1][cols(h), :] = dot(q_ref[:, cols(h)], g_ref[:, cols(h)], 0, 0).astype(BF16)


def plane_kernel(ids, *refs):
    for o, ref in enumerate(refs[:-1]):
        refs[-1][span(ids[2] ^ o, ref.shape[0]), :] = ref[...]


def slot_state_kernel(slots, ids, left_ref, *refs):
    rights, (out_ref, whole_ref) = refs[:slots], refs[-2:]
    block = rights[0].shape[1]
    for o, right_ref in enumerate(rights):
        b = ids[0] ^ o
        left = left_ref[:, span(b, block)]
        whole_ref[:, span(b, block)] = right_ref[...]
        for j in range(block // HEAD):
            state = dot(left[:, cols(j)], right_ref[:, cols(j)], 0, 0).astype(BF16)
            out_ref[span(b * (block // HEAD) + j, HEAD), :] = state


def prefix_kernel(reverse, ids, part_ref, *refs):
    out_ref = refs[-1]
    count = part_ref.shape[0]
    total = jnp.zeros(out_ref.shape[1:], F32)
    for step in range(count):
        i = count - 1 - step if reverse else step
        out_ref[i] = total.astype(BF16)
        total = total + part_ref[i, :, :HEAD].astype(F32)


def values_kernel(slots, planes, ids, x_ref, *refs):
    pieces, outs, (w_ref, res_ref) = refs[:planes], refs[-slots - 2:-2], refs[-2:]
    step = pl.program_id(0)
    count, rows = x_ref.shape[:2]

    @pl.when(step == 0)
    def _():
        for o, piece in enumerate(pieces):
            w_ref[span(ids[1] ^ o, piece.shape[0]), :] = piece[...]

    x = x_ref[...].reshape(count * rows, x_ref.shape[2])
    res_ref[...] = dot(x, w_ref[...], 1, 0).astype(BF16).reshape(res_ref.shape)
    for o, out_ref in enumerate(outs):
        @pl.when(step == o // count)
        def _(o=o, out_ref=out_ref):
            out_ref[...] = res_ref[(ids[0] ^ o) % count]


def grad_values_kernel(scale, slots, ids, q_ref, k_ref, g_ref, qg_ref, *refs):
    outs = refs[-slots:]
    mask = causal_mask(q_ref.shape[0])
    block = outs[0].shape[1]
    for o, out_ref in enumerate(outs):
        b = ids[0] ^ o
        at = span(b, block)
        qs, ks, gs = q_ref[:, at], k_ref[:, at], g_ref[:, at]
        for j in range(block // HEAD):
            q, k, g = qs[:, cols(j)], ks[:, cols(j)], gs[:, cols(j)]
            state = qg_ref[span(b * (block // HEAD) + j, HEAD), :]
            score = jnp.where(mask, dot(q, k, 1, 1) * scale, 0.0).astype(BF16)
            grad = scale * dot(k, state, 1, 0) + dot(score, g, 0, 0)
            out_ref[:, cols(j)] = grad.astype(BF16)


def grad_key_kernel(scale, ids, q_ref, g_ref, v_ref, qg_ref, *refs):
    gk_ref, score_ref = refs[-2:]
    mask = causal_mask(q_ref.shape[0])
    for h in range(q_ref.shape[1] // HEAD):
        q, g, v = q_ref[:, cols(h)], g_ref[:, cols(h)], v_ref[:, cols(h)]
        score = jnp.where(mask, dot(g, v, 1, 1) * scale, 0.0).astype(BF16)
        score_ref[cols(h), :] = score
        grad = scale * dot(v, qg_ref[cols(h), :], 1, 1) + dot(score, q, 0, 0)
        gk_ref[:, cols(h)] = grad.astype(BF16)


def grad_query_kernel(scale, ids, k_ref, g_ref, score_ref, kv_ref, gq_ref):
    for h in range(k_ref.shape[1] // HEAD):
        grad = scale * dot(g_ref[:, cols(h)], kv_ref[cols(h), :], 1, 1)
        grad = grad + dot(score_ref[cols(h), :], k_ref[:, cols(h)], 1, 0)
        gq_ref[:, cols(h)] = grad.astype(BF16)


def product_kernel(slots, ids, x_ref, *refs):
    pieces, out_ref, held_ref = refs[:slots], refs[-2], refs[-1]

    @pl.when(pl.program_id(0) == 0)
    def _():
        for o, piece in enumerate(pieces):
            held_ref[:, span(ids[0] ^ o, piece.shape[0])] = piece[...].T

    out_ref[0] = dot(held_ref[...], x_ref[...], 1, 0).astype(BF16).T


def parts_sum_kernel(factor, ids, part_ref, *refs):
    total = part_ref[0].astype(F32)
    for i in range(1, part_ref.shape[0]):
        total = total + part_ref[i].astype(F32)
    refs[-1][...] = (total * factor).astype(BF16)


def assemble_kernel(ids, part_ref, out_ref):
    block = part_ref.shape[2]
    for b in range(part_ref.shape[0]):
        out_ref[:, b * block:(b + 1) * block] = part_ref[b].astype(F32)


def call(kernel, shapes, flops, ids, *operands, grid=None, first=None, out_first=None, scratch=(), after=(), through=()):
    out = [jax.ShapeDtypeStruct(s, d) for s, d in shapes]
    moved = sum(x.size * x.dtype.itemsize for x in list(operands) + out)
    whole = lambda s: pl.BlockSpec(s, lambda *_: (0,) * len(s))
    anywhere = pl.BlockSpec(memory_space=pl.ANY)
    in_specs = [whole(x.shape) for x in operands]
    if first is not None:
        in_specs[0] = first
    out_specs = [out_first] if out_first else [whole(s) for s, _ in shapes]
    result = pl.pallas_call(
        kernel,
        out_shape=[jax.ShapeDtypeStruct(x.shape, x.dtype) for x in through] + out,
        grid_spec=pltpu.PrefetchScalarGridSpec(
            num_scalar_prefetch=1,
            grid=grid or (1,),
            in_specs=in_specs + [anywhere] * (len(after) + len(through)),
            out_specs=[anywhere] * len(through) + out_specs,
            scratch_shapes=list(scratch),
        ),
        input_output_aliases={1 + len(operands) + len(after) + i: i for i in range(len(through))},
        compiler_params=pltpu.CompilerParams(vmem_limit_bytes=16 * 2**20),
        cost_estimate=pl.CostEstimate(flops=flops, bytes_accessed=moved, transcendentals=0),
    )(ids, *operands, *after, *through)
    return result[0] if len(result) == 1 else result


def on_device(inputs, query_rows, key_rows, cotangent, w_value):
    rows, width = inputs.shape[1:]
    width_all = query_rows.shape[2]
    heads = width_all // HEAD
    seq, dp = lax.axis_size("seq"), lax.axis_size("dp")
    y_count = seq // Z
    planes = [[y * Z + z for z in range(Z)] for y in range(y_count)]
    columns = [[y * Z + z for y in range(y_count)] for z in range(Z)]
    scale = 1.0 / math.sqrt(HEAD * rows * seq)
    grad_scale = 1.0 / math.sqrt(inputs.shape[0] * dp * rows * seq)
    block = width_all // dp
    q, k, g = query_rows[0], key_rows[0], cotangent[0]
    head_flops = 2 * rows * HEAD * HEAD * heads
    at_dp, at_seq = lax.axis_index("dp"), lax.axis_index("seq")
    ids = jnp.stack([at_dp, at_seq // Z, at_seq % Z]).astype(jnp.int32)


    def exchange(array, groups=None):
        return lax.all_to_all(array, "seq", 0, 0, axis_index_groups=groups, tiled=True)

    def swap_slots(arrays, axis="dp", stride=1):
        count = lax.axis_size(axis)
        return [
            a if o == 0 else lax.ppermute(a, axis, [(i, i ^ (o * stride)) for i in range(count)])
            for o, a in enumerate(arrays)
        ]

    def sums_of(parts, reverse, through=(), after=()):
        return call(
            functools.partial(prefix_kernel, reverse), [((seq, width_all // seq, HEAD), BF16)],
            seq * width_all // seq * HEAD, ids, parts, through=through, after=after,
        )

    all_inputs = lax.all_gather(inputs, "dp", axis=0, tiled=True)

    own = lax.dynamic_slice_in_dim(w_value, at_dp * block, block, 1)
    plane = call(
        plane_kernel, [((Z * own.shape[0], block), BF16)], 0, ids, *swap_slots([own] * Z, "seq")
    )
    pieces = swap_slots([plane] * y_count, "seq", Z)
    qg_local = call(
        state_kernel, [((width_all, HEAD), BF16)], head_flops, ids, q, g, after=(plane,)
    )
    qg_parts = exchange(qg_local.reshape(seq, -1, HEAD))
    qg_sums = sums_of(qg_parts, True, after=tuple(pieces[1:]))
    qg_round = exchange(qg_sums).reshape(width_all, HEAD)

    values = call(
        functools.partial(values_kernel, dp, y_count), [((rows, block), BF16)] * dp,
        2 * rows * width * width_all, ids, all_inputs, *pieces, after=(qg_sums,),
        grid=(dp // 2,),
        first=pl.BlockSpec((2, rows, width), lambda i, ids: ((ids[0] // 2) ^ i, 0, 0)),
        scratch=[pltpu.VMEM((width, block), BF16), pltpu.VMEM((2, rows, block), BF16)],
    )
    kv_local, values = call(
        functools.partial(slot_state_kernel, dp),
        [((heads * HEAD, HEAD), BF16), ((rows, width_all), BF16)], head_flops, ids, k,
        *swap_slots(values), after=(qg_round,),
    )
    kv_parts = exchange(kv_local.reshape(seq, -1, HEAD))

    grad_values = call(
        functools.partial(grad_values_kernel, scale, dp), [((rows, block), BF16)] * dp,
        3 * head_flops, ids, q, k, g, qg_round, after=(kv_local,),
    )
    terms = call(
        functools.partial(product_kernel, dp), [((y_count, width // y_count, block), BF16)],
        2 * rows * width * width_all, ids, all_inputs.reshape(dp * rows, width),
        *swap_slots(grad_values),
        grid=(y_count,),
        first=pl.BlockSpec((dp * rows, width // y_count), lambda i, ids: (0, i)),
        out_first=pl.BlockSpec((1, width // y_count, block), lambda i, ids: (i, 0, 0)),
        scratch=[pltpu.VMEM((block, dp * rows), BF16)],
    )
    terms, kv_sums = sums_of(kv_parts, False, (terms,))
    grad_key, score = call(
        functools.partial(grad_key_kernel, scale),
        [((rows, width_all), BF16), ((heads * HEAD, rows), BF16)],
        3 * head_flops, ids, q, g, values, qg_round, after=(kv_sums,),
    )
    kv_round = exchange(kv_sums).reshape(width_all, HEAD)
    term = lax.psum_scatter(
        terms.reshape(width, block), "seq", scatter_dimension=0, axis_index_groups=columns, tiled=True
    )
    parts = exchange(term.reshape(Z, width // seq, block), planes)
    summed = call(
        functools.partial(parts_sum_kernel, grad_scale), [((width // seq, block), BF16)],
        0, ids, parts, after=(kv_round, score),
    )
    grad_weight = call(
        assemble_kernel, [((width // seq, width_all), F32)], 0, ids, lax.all_gather(summed, "dp")
    )

    grad_query = call(
        functools.partial(grad_query_kernel, scale), [((rows, width_all), BF16)],
        2 * head_flops, ids, k, g, score, kv_round,
    )
    return grad_query[None], grad_key[None], grad_weight


def solution(mesh):
    placed = (
        P("dp", "seq", None),
        P("dp", "seq", None),
        P("dp", "seq", None),
        P("dp", "seq", None),
        P("seq", None),
    )
    return jax.shard_map(
        on_device,
        mesh=mesh,
        in_specs=placed,
        out_specs=(P("dp", "seq", None), P("dp", "seq", None), P("seq", None)),
        check_vma=False,
    )
```

```python
import functools
import math

import jax
import jax.numpy as jnp
from jax import lax
from jax.experimental import pallas as pl
from jax.experimental.pallas import tpu as pltpu
from jax.sharding import PartitionSpec as P

HEAD = 128
Z = 8
F32 = jnp.float32
BF16 = jnp.bfloat16


def dot(a, b, a_dim, b_dim):
    return lax.dot_general(a, b, (((a_dim,), (b_dim,)), ((), ())), preferred_element_type=F32)


def cols(h):
    return slice(h * HEAD, (h + 1) * HEAD)


def span(index, size):
    return pl.ds(pl.multiple_of(index * size, size), size)


def causal_mask(rows):
    t = lax.broadcasted_iota(jnp.int32, (rows, rows), 0)
    s = lax.broadcasted_iota(jnp.int32, (rows, rows), 1)
    return t >= s


def first_kernel(ids, q_ref, g_ref, w_ref, out_ref):
    count, rows, _ = out_ref.shape
    for h in range(q_ref.shape[1] // HEAD):
        state = dot(q_ref[:, cols(h)], g_ref[:, cols(h)], 0, 0).astype(BF16)
        for i in range(HEAD // rows):
            out_ref[h * (HEAD // rows) + i, :, :HEAD] = state[i * rows:(i + 1) * rows, :]
    block = out_ref.shape[2] - HEAD
    own = w_ref[:, span(ids[0], block)]
    for i in range(count):
        out_ref[i, :, HEAD:] = own


def slot_state_kernel(slots, ids, left_ref, *refs):
    rights, (out_ref, whole_ref) = refs[:slots], refs[-2:]
    block = rights[0].shape[1]
    for o, right_ref in enumerate(rights):
        b = ids[0] ^ o
        left = left_ref[:, span(b, block)]
        whole_ref[:, span(b, block)] = right_ref[...]
        for j in range(block // HEAD):
            state = dot(left[:, cols(j)], right_ref[:, cols(j)], 0, 0).astype(BF16)
            out_ref[span(b * (block // HEAD) + j, HEAD), :] = state


def prefix_kernel(reverse, ids, part_ref, *refs):
    out_ref = refs[-1]
    count = part_ref.shape[0]
    total = jnp.zeros(out_ref.shape[1:], F32)
    for step in range(count):
        i = count - 1 - step if reverse else step
        out_ref[i] = total.astype(BF16)
        total = total + part_ref[i, :, :HEAD].astype(F32)


def values_kernel(slots, ids, x_ref, first_ref, *refs):
    outs, (w_ref, res_ref) = refs[-slots - 2:-2], refs[-2:]
    step = pl.program_id(0)
    count, rows = x_ref.shape[:2]

    @pl.when(step == 0)
    def _():
        size = first_ref.shape[1]
        for i in range(first_ref.shape[0]):
            w_ref[i * size:(i + 1) * size, :] = first_ref[i, :, HEAD:]

    x = x_ref[...].reshape(count * rows, x_ref.shape[2])
    res_ref[...] = dot(x, w_ref[...], 1, 0).astype(BF16).reshape(res_ref.shape)
    for o, out_ref in enumerate(outs):
        @pl.when(step == o // count)
        def _(o=o, out_ref=out_ref):
            out_ref[...] = res_ref[(ids[0] ^ o) % count]


def grad_values_kernel(scale, slots, ids, q_ref, k_ref, g_ref, qg_ref, *refs):
    outs = refs[-slots:]
    mask = causal_mask(q_ref.shape[0])
    block = outs[0].shape[1]
    for o, out_ref in enumerate(outs):
        b = ids[0] ^ o
        at = span(b, block)
        qs, ks, gs = q_ref[:, at], k_ref[:, at], g_ref[:, at]
        for j in range(block // HEAD):
            q, k, g = qs[:, cols(j)], ks[:, cols(j)], gs[:, cols(j)]
            state = qg_ref[span(b * (block // HEAD) + j, HEAD), :]
            score = jnp.where(mask, dot(q, k, 1, 1) * scale, 0.0).astype(BF16)
            grad = scale * dot(k, state, 1, 0) + dot(score, g, 0, 0)
            out_ref[:, cols(j)] = grad.astype(BF16)


def grad_key_kernel(scale, ids, q_ref, g_ref, v_ref, qg_ref, *refs):
    gk_ref, score_ref = refs[-2:]
    mask = causal_mask(q_ref.shape[0])
    for h in range(q_ref.shape[1] // HEAD):
        q, g, v = q_ref[:, cols(h)], g_ref[:, cols(h)], v_ref[:, cols(h)]
        score = jnp.where(mask, dot(g, v, 1, 1) * scale, 0.0).astype(BF16)
        score_ref[cols(h), :] = score
        grad = scale * dot(v, qg_ref[cols(h), :], 1, 1) + dot(score, q, 0, 0)
        gk_ref[:, cols(h)] = grad.astype(BF16)


def grad_query_kernel(scale, ids, k_ref, g_ref, score_ref, kv_ref, gq_ref):
    for h in range(k_ref.shape[1] // HEAD):
        grad = scale * dot(g_ref[:, cols(h)], kv_ref[cols(h), :], 1, 1)
        grad = grad + dot(score_ref[cols(h), :], k_ref[:, cols(h)], 1, 0)
        gq_ref[:, cols(h)] = grad.astype(BF16)


def product_kernel(slots, ids, x_ref, *refs):
    pieces, out_ref, held_ref = refs[:slots], refs[-2], refs[-1]

    @pl.when(pl.program_id(0) == 0)
    def _():
        for o, piece in enumerate(pieces):
            held_ref[:, span(ids[0] ^ o, piece.shape[0])] = piece[...].T

    out_ref[0] = dot(held_ref[...], x_ref[...], 1, 0).astype(BF16).T


def parts_sum_kernel(factor, ids, part_ref, *refs):
    total = part_ref[0].astype(F32)
    for i in range(1, part_ref.shape[0]):
        total = total + part_ref[i].astype(F32)
    refs[-1][...] = (total * factor).astype(BF16)


def assemble_kernel(ids, part_ref, out_ref):
    block = part_ref.shape[2]
    for b in range(part_ref.shape[0]):
        out_ref[:, b * block:(b + 1) * block] = part_ref[b].astype(F32)


def call(kernel, shapes, flops, ids, *operands, grid=None, first=None, out_first=None, scratch=(), after=(), through=()):
    out = [jax.ShapeDtypeStruct(s, d) for s, d in shapes]
    moved = sum(x.size * x.dtype.itemsize for x in list(operands) + out)
    whole = lambda s: pl.BlockSpec(s, lambda *_: (0,) * len(s))
    anywhere = pl.BlockSpec(memory_space=pl.ANY)
    in_specs = [whole(x.shape) for x in operands]
    if first is not None:
        in_specs[0] = first
    out_specs = [out_first] if out_first else [whole(s) for s, _ in shapes]
    result = pl.pallas_call(
        kernel,
        out_shape=[jax.ShapeDtypeStruct(x.shape, x.dtype) for x in through] + out,
        grid_spec=pltpu.PrefetchScalarGridSpec(
            num_scalar_prefetch=1,
            grid=grid or (1,),
            in_specs=in_specs + [anywhere] * (len(after) + len(through)),
            out_specs=[anywhere] * len(through) + out_specs,
            scratch_shapes=list(scratch),
        ),
        input_output_aliases={1 + len(operands) + len(after) + i: i for i in range(len(through))},
        compiler_params=pltpu.CompilerParams(vmem_limit_bytes=16 * 2**20),
        cost_estimate=pl.CostEstimate(flops=flops, bytes_accessed=moved, transcendentals=0),
    )(ids, *operands, *after, *through)
    return result[0] if len(result) == 1 else result


def on_device(inputs, query_rows, key_rows, cotangent, w_value):
    rows, width = inputs.shape[1:]
    width_all = query_rows.shape[2]
    heads = width_all // HEAD
    seq, dp = lax.axis_size("seq"), lax.axis_size("dp")
    y_count = seq // Z
    planes = [[y * Z + z for z in range(Z)] for y in range(y_count)]
    columns = [[y * Z + z for y in range(y_count)] for z in range(Z)]
    scale = 1.0 / math.sqrt(HEAD * rows * seq)
    grad_scale = 1.0 / math.sqrt(inputs.shape[0] * dp * rows * seq)
    block = width_all // dp
    q, k, g = query_rows[0], key_rows[0], cotangent[0]
    head_flops = 2 * rows * HEAD * HEAD * heads
    ids = lax.axis_index("dp").astype(jnp.int32)[None]


    def exchange(array, groups=None):
        return lax.all_to_all(array, "seq", 0, 0, axis_index_groups=groups, tiled=True)

    def swap_slots(arrays):
        return [
            a if o == 0 else lax.ppermute(a, "dp", [(i, i ^ o) for i in range(dp)])
            for o, a in enumerate(arrays)
        ]

    def sums_of(parts, reverse, through=()):
        return call(
            functools.partial(prefix_kernel, reverse), [((seq, width_all // seq, HEAD), BF16)],
            seq * width_all // seq * HEAD, ids, parts, through=through,
        )

    all_inputs = lax.all_gather(inputs, "dp", axis=0, tiled=True)

    first = exchange(call(
        first_kernel, [((seq, width // seq, HEAD + block), BF16)], head_flops, ids, q, g, w_value
    ))
    qg_sums = sums_of(first, True)
    qg_round = exchange(qg_sums).reshape(width_all, HEAD)

    values = call(
        functools.partial(values_kernel, dp), [((rows, block), BF16)] * dp,
        2 * rows * width * width_all, ids, all_inputs, first, after=(qg_sums,),
        grid=(dp // 2,),
        first=pl.BlockSpec((2, rows, width), lambda i, ids: ((ids[0] // 2) ^ i, 0, 0)),
        scratch=[pltpu.VMEM((width, block), BF16), pltpu.VMEM((2, rows, block), BF16)],
    )
    grad_values = call(
        functools.partial(grad_values_kernel, scale, dp), [((rows, block), BF16)] * dp,
        3 * head_flops, ids, q, k, g, qg_round,
    )
    kv_local, values = call(
        functools.partial(slot_state_kernel, dp),
        [((heads * HEAD, HEAD), BF16), ((rows, width_all), BF16)], head_flops, ids, k,
        *swap_slots(values), after=(grad_values[0],),
    )
    kv_parts = exchange(kv_local.reshape(seq, -1, HEAD))

    terms = call(
        functools.partial(product_kernel, dp), [((y_count, width // y_count, block), BF16)],
        2 * rows * width * width_all, ids, all_inputs.reshape(dp * rows, width),
        *swap_slots(grad_values),
        grid=(y_count,),
        first=pl.BlockSpec((dp * rows, width // y_count), lambda i, ids: (0, i)),
        out_first=pl.BlockSpec((1, width // y_count, block), lambda i, ids: (i, 0, 0)),
        scratch=[pltpu.VMEM((block, dp * rows), BF16)],
    )
    terms, kv_sums = sums_of(kv_parts, False, (terms,))
    grad_key, score = call(
        functools.partial(grad_key_kernel, scale),
        [((rows, width_all), BF16), ((heads * HEAD, rows), BF16)],
        3 * head_flops, ids, q, g, values, qg_round, after=(kv_sums,),
    )
    kv_round = exchange(kv_sums).reshape(width_all, HEAD)
    term = lax.psum_scatter(
        terms.reshape(width, block), "seq", scatter_dimension=0, axis_index_groups=columns, tiled=True
    )
    parts = exchange(term.reshape(Z, width // seq, block), planes)
    summed = call(
        functools.partial(parts_sum_kernel, grad_scale), [((width // seq, block), BF16)],
        0, ids, parts, after=(kv_round, score),
    )
    grad_weight = call(
        assemble_kernel, [((width // seq, width_all), F32)], 0, ids, lax.all_gather(summed, "dp")
    )

    grad_query = call(
        functools.partial(grad_query_kernel, scale), [((rows, width_all), BF16)],
        2 * head_flops, ids, k, g, score, kv_round,
    )
    return grad_query[None], grad_key[None], grad_weight


def solution(mesh):
    placed = (
        P("dp", "seq", None),
        P("dp", "seq", None),
        P("dp", "seq", None),
        P("dp", "seq", None),
        P("seq", None),
    )
    return jax.shard_map(
        on_device,
        mesh=mesh,
        in_specs=placed,
        out_specs=(P("dp", "seq", None), P("dp", "seq", None), P("seq", None)),
        check_vma=False,
    )
```
